512 devices in a mesh: dp: 64 (over z_lo, y, core), seq: 8 (over z_hi, x).
Axes of the slice: x: 4, y: 4, z: 16 (z_hi: 2, z_lo: 8; z = z_hi * 8 + z_lo), core: 2. Of those that a mesh axis runs over, the one named last changes fastest.
Arguments:
- hidden_in: bfloat16 [65536, 2048], P(('dp', 'seq')), may hold values from -6 to 6
- norm_gain: float32 [2048], replicated, may hold values from 0.5 to 1.5
- resid_grad: bfloat16 [65536, 2048], P(('dp', 'seq')), may hold values from -3 to 3
- key_output_gradient: bfloat16 [65536, 512], P('dp', 'seq'), may hold values from -6 to 6
- value_output_gradient: bfloat16 [65536, 512], P('dp', 'seq'), may hold values from -6 to 6
- key_matrix: bfloat16 [2048, 512], P(None, 'seq'), may hold values from -0.125 to 0.125
- value_matrix: bfloat16 [2048, 512], P(None, 'seq'), may hold values from -0.125 to 0.125
Outputs:
- input_grad: bfloat16 [65536, 2048], P(('dp', 'seq'))
- key_weight_grad: float32 [2048, 512], P('dp', 'seq')
- value_weight_grad: float32 [2048, 512], P('dp', 'seq')
- gain_grad: float32 [2048], replicated
The draws below stay inside these ranges and needn't reach their ends.
All inputs are finite; a program needn't handle non-finite values.
Results may differ from the reference program's by a relative error of at most 0.0029.
Values may be sent and summed in bfloat16 or wider, within the bound.
A program may use at most 64 MiB of HBM per device.

```python
import math
import jax
import jax.numpy as jnp
from jax import lax

MODEL_DIMENSION = 2048
KEY_VALUE_HEADS = 4
HEAD_SIZE = 128
TOKEN_COUNT = 65536


def block_scale(rng, extent, cuts, smallest, top_value):
    def one(axis_at, blocks):
        draws = jax.random.uniform(jax.random.fold_in(jax.random.fold_in(rng, 6), axis_at), (blocks,), jnp.float32, smallest / len(cuts), top_value / len(cuts))
        return jnp.repeat(jnp.exp(draws), extent[axis_at] // blocks).reshape((-1,) + (1,) * (len(extent) - axis_at - 1))

    level = one(*cuts[0])
    for cut in cuts[1:]:
        level = level * one(*cut)
    return level


def noise(key, extent, width, bound, split=(), held_as=jnp.bfloat16):
    drawn = jax.random.normal(key, extent, jnp.float32) * width
    if len(split) > 0:
        drawn = block_scale(key, extent, split, -0.22, 0.18) * drawn
    return jnp.clip(drawn, min=-bound, max=bound).astype(held_as)


def setup_inputs(seed: int = 0) -> dict:
    streams_of = jax.random.split(jax.random.key(seed), 8)
    return {
        "hidden_in": noise(streams_of[0], (TOKEN_COUNT, MODEL_DIMENSION), 1.0, 6.0, ((0, 512),)),
        "norm_gain": jnp.clip(1.0 + 0.1 * jax.random.normal(streams_of[1], (MODEL_DIMENSION,), jnp.float32), 0.5, 1.5),
        "resid_grad": noise(streams_of[2], (TOKEN_COUNT, MODEL_DIMENSION), 0.5, 3.0, ((0, 512),)),
        "key_output_gradient": noise(streams_of[3], (TOKEN_COUNT, KEY_VALUE_HEADS * HEAD_SIZE), 1.0, 6.0, ((0, 64), (1, 8))),
        "value_output_gradient": noise(streams_of[4], (TOKEN_COUNT, KEY_VALUE_HEADS * HEAD_SIZE), 1.0, 6.0, ((0, 64), (1, 8))),
        "key_matrix": noise(streams_of[5], (MODEL_DIMENSION, KEY_VALUE_HEADS * HEAD_SIZE), MODEL_DIMENSION ** -0.5, 0.125, ((1, 8),)),
        "value_matrix": noise(streams_of[6], (MODEL_DIMENSION, KEY_VALUE_HEADS * HEAD_SIZE), MODEL_DIMENSION ** -0.5, 0.125, ((1, 8),)),
    }


def reference(hidden_in, norm_gain, resid_grad, key_output_gradient, value_output_gradient, key_matrix, value_matrix):
    scale = 1.0 / math.sqrt(TOKEN_COUNT)
    widened = hidden_in.astype(jnp.float32)
    inv_rms = lax.rsqrt(lax.optimization_barrier(jnp.mean(widened * widened, axis=-1, keepdims=True)) + 1e-05)
    unit_rows = widened * inv_rms
    normed = (unit_rows * norm_gain).astype(jnp.bfloat16)
    key_weight_grad = jnp.dot(normed.T, key_output_gradient, preferred_element_type=jnp.float32) * scale
    value_weight_grad = jnp.dot(normed.T, value_output_gradient, preferred_element_type=jnp.float32) * scale
    normed_grad = jnp.dot(key_output_gradient, key_matrix.T, preferred_element_type=jnp.float32)
    normed_grad = normed_grad + jnp.dot(value_output_gradient, value_matrix.T, preferred_element_type=jnp.float32)
    gain_grad = lax.optimization_barrier(jnp.sum(normed_grad * unit_rows, axis=0)) * scale
    scaled = normed_grad * norm_gain
    inner = lax.optimization_barrier(jnp.mean(scaled * unit_rows, axis=-1, keepdims=True))
    input_grad = (resid_grad.astype(jnp.float32) + inv_rms * (scaled - unit_rows * inner)).astype(jnp.bfloat16)
    return (input_grad, key_weight_grad, value_weight_grad, gain_grad)
```

```python
import functools
import math

import jax
import jax.numpy as jnp
from jax import lax
from jax.experimental import pallas as pl
from jax.experimental.pallas import tpu as pltpu
from jax.sharding import PartitionSpec as P

EPSILON = 1e-05
MESH = pl.DeviceIdType.MESH
BF16, F32 = jnp.bfloat16, jnp.float32
NX, NY, NZL, NZH, NC = 4, 4, 8, 2, 2
NT_DIMS = (((1,), (1,)), ((), ()))


def kernel(
    scale,
    hid_hbm,
    gain_hbm,
    res_hbm,
    kt_hbm,
    vt_hbm,
    wk_hbm,
    wv_hbm,
    out_ref,
    kw_ref,
    vw_ref,
    gain_out,
    hid,
    res,
    gain,
    inv_ref,
    nrm,
    nt,
    ng_all,
    kv,
    kv_far,
    kv_tok,
    w_all,
    normed_grad,
    y_send,
    y_recv,
    own_sum,
    z_send,
    z_recv,
    ga,
    g1,
    g2,
    g3,
    gf,
    load_sem,
    wz_s,
    wz_r,
    wx_s,
    wx_r,
    wy_s,
    wy_r,
    wc_s,
    wc_r,
    kz_s,
    kz_r,
    kc_s,
    kc_r,
    kx_s,
    kx_r,
    n_s,
    n_r,
    y_s,
    y_r,
    z_s,
    z_r,
    g1_s,
    g1_r,
    g2_s,
    g2_r,
    g3_s,
    g3_r,
    g4_s,
    g4_r,
):
    dp, sq = lax.axis_index("dp"), lax.axis_index("seq")
    c, y, zl = dp % NC, (dp // NC) % NY, dp // (NC * NY)
    x, zh = sq % NX, sq // NX
    z = zh * NZL + zl
    nz = NZL * NZH
    rows, width = hid.shape
    cols = wk_hbm.shape[0]
    half = rows * NX
    piece = width // (NY * NC)

    def device(dc=0, dx=0, dy=0, zz=None):
        cc, xx, yy = (c + dc) % NC, (x + dx) % NX, (y + dy) % NY
        zz = z if zz is None else zz
        return ((zz % NZL) * NY + yy) * NC + cc, (zz // NZL) * NX + xx

    def remote(src, dst, ssem, rsem, to):
        return pltpu.make_async_remote_copy(
            src_ref=src, dst_ref=dst, send_sem=ssem, recv_sem=rsem, device_id=to, device_id_type=MESH
        )

    def aligned(index, size):
        return pl.ds(pl.multiple_of(index * size, size), size)

    near, far = aligned(zh, half), aligned(1 - zh, half)
    loads = [
        pltpu.make_async_copy(hid_hbm, hid, load_sem.at[0]),
        pltpu.make_async_copy(gain_hbm, gain, load_sem.at[1]),
        pltpu.make_async_copy(kt_hbm.at[:, far], kv_far.at[pl.ds(0, cols)], load_sem.at[2]),
        pltpu.make_async_copy(vt_hbm.at[:, far], kv_far.at[pl.ds(cols, cols)], load_sem.at[3]),
        pltpu.make_async_copy(wk_hbm, w_all.at[0, pl.ds(0, cols)], load_sem.at[4]),
        pltpu.make_async_copy(wv_hbm, w_all.at[0, pl.ds(cols, cols)], load_sem.at[5]),
        pltpu.make_async_copy(kt_hbm.at[:, near], kv.at[0, pl.ds(0, cols)], load_sem.at[6]),
        pltpu.make_async_copy(vt_hbm.at[:, near], kv.at[0, pl.ds(cols, cols)], load_sem.at[7]),
        pltpu.make_async_copy(res_hbm, res, load_sem.at[8]),
    ]
    for load in loads:
        load.start()

    barrier = pltpu.get_barrier_semaphore()
    xc = [(dx, dc) for dx in range(NX) for dc in range(NC) if dx or dc]
    peers = [device(dc=dc, dx=dx) for dx, dc in xc]
    peers += [device(dy=dy) for dy in range(1, NY)]
    peers += [device(zz=(z + dz) % nz) for dz in range(1, nz)]
    for peer in peers:
        pl.semaphore_signal(barrier, inc=1, device_id=peer, device_id_type=MESH)

    loads[0].wait()
    loads[1].wait()
    step = 16
    for at in range(0, rows, step):
        wide = hid[at : at + step].astype(F32)
        inv = lax.rsqrt(jnp.mean(wide * wide, axis=-1, keepdims=True) + EPSILON)
        inv_ref[at : at + step] = inv
        nrm[at : at + step] = (wide * inv * gain[...]).astype(BF16)
    block = width // (NC * NY * NZL)
    lane = min(128, width)
    for at in range(0, width, lane):
        turned = nrm[:, at : at + lane].T
        for part in range(lane // block):
            b = at // block + part
            bc, by, bz = b % NC, (b // NC) % NY, b // (NC * NY)
            nt[bc, by, bz * block : (bz + 1) * block] = turned[part * block : (part + 1) * block]
    for load in loads[2:8]:
        load.wait()
    pl.semaphore_wait(barrier, len(peers))

    q = aligned(c * NY + y, piece)
    sends = []

    def go(copy):
        copy.start()
        sends.append(copy)
        return copy

    w_z = go(remote(w_all.at[0, :, q], w_all.at[NX, :, q], wz_s, wz_r, device(zz=nz - 1 - z)))
    k_z = go(remote(kv_far, kv.at[0, pl.ds(2 * cols, 2 * cols)], kz_s, kz_r, device(zz=(z + nz // 2) % nz)))
    w_x = [
        go(remote(w_all.at[0, :, q], w_all.at[dx, :, q], wx_s.at[dx - 1], wx_r.at[dx - 1], device(dx=dx)))
        for dx in range(1, NX)
    ]
    k_c = go(remote(kv.at[0, pl.ds(0, 2 * cols)], kv.at[1, pl.ds(0, 2 * cols)], kc_s.at[0], kc_r.at[0], device(dc=1)))

    def token_sends(rel):
        return [
            go(
                remote(
                    kv.at[0, pl.ds(rel * 2 * cols, 2 * cols), aligned((x + dx) % NX, rows)],
                    kv_tok.at[rel * NX + dx],
                    kx_s.at[rel * NX + dx],
                    kx_r.at[rel * NX + dx],
                    device(dx=dx),
                )
            )
            for dx in range(1, NX)
        ]

    k_x = token_sends(0)
    mine = aligned(x, rows)
    n_all = []
    for i, (dx, dc) in enumerate(xc):
        n_all.append(
            go(remote(nt.at[(c + dc) % NC], ng_all.at[dc, :, :, mine], n_s.at[i], n_r.at[i], device(dc=dc, dx=dx)))
        )
    own = pltpu.make_async_copy(nt.at[c], ng_all.at[0, :, :, mine], load_sem.at[9])
    own.start()

    def y_sends(first, count, rel):
        return [
            go(
                remote(
                    w_all.at[pl.ds(first, count), :, q],
                    w_all.at[pl.ds(first, count), :, q],
                    wy_s.at[rel * NY + dy],
                    wy_r.at[rel * NY + dy],
                    device(dy=dy),
                )
            )
            for dy in range(1, NY)
        ]

    for copy in w_x:
        copy.wait_recv()
    w_y = y_sends(1, NX - 1, 0)
    w_z.wait_recv()
    w_x2 = [
        go(
            remote(
                w_all.at[NX, :, q],
                w_all.at[NX + dx, :, q],
                wx_s.at[NX - 1 + dx - 1],
                wx_r.at[NX - 1 + dx - 1],
                device(dx=dx),
            )
        )
        for dx in range(1, NX)
    ]
    for copy in w_x2:
        copy.wait_recv()
    w_y2 = y_sends(NX, NX, 1)

    k_z.wait_recv()
    k_c2 = go(
        remote(
            kv.at[0, pl.ds(2 * cols, 2 * cols)],
            kv.at[1, pl.ds(2 * cols, 2 * cols)],
            kc_s.at[1],
            kc_r.at[1],
            device(dc=1),
        )
    )
    k_x += token_sends(1)
    own.wait()
    for copy in n_all:
        copy.wait_recv()
    k_c.wait_recv()
    k_c2.wait_recv()

    y_all = []
    for dy in [d for d in (2, 1, 3, 0) if d < NY]:
        to = (y + dy) % NY
        total = lax.dot_general(ng_all[0, to], kv[0], NT_DIMS, preferred_element_type=F32)
        total = total + lax.dot_general(ng_all[1, to], kv[1], NT_DIMS, preferred_element_type=F32)
        if dy:
            y_send[dy - 1] = total.astype(BF16)
            y_all.append(go(remote(y_send.at[dy - 1], y_recv.at[dy - 1], y_s.at[dy - 1], y_r.at[dy - 1], device(dy=dy))))
        else:
            own_sum[...] = total

    side = aligned(c, width // NC)
    for copy in w_y + w_y2:
        copy.wait_recv()
    w_c = go(
        remote(w_all.at[pl.ds(1, 2 * NX - 1), :, side], w_all.at[pl.ds(1, 2 * NX - 1), :, side], wc_s, wc_r, device(dc=1))
    )

    for copy in y_all:
        copy.wait_recv()
    total = own_sum[...]
    for i in range(NY - 1):
        total = total + y_recv[i].astype(F32)
    own_sum[...] = total
    for rel in range(NZH):
        z_send[rel] = total[:, rel * 2 * cols : (rel + 1) * 2 * cols].astype(BF16)
    z_all = []
    for dz in sorted(range(1, nz), key=lambda d: -min(d, nz - d)):
        to = (z + dz) % nz
        z_all.append(
            go(
                remote(
                    z_send.at[(to // NZL + zh) % NZH, aligned(to % NZL, block)],
                    z_recv.at[dz - 1],
                    z_s.at[dz - 1],
                    z_r.at[dz - 1],
                    device(zz=to),
                )
            )
        )

    for copy in k_x:
        copy.wait_recv()
    for rel in range(NZH):
        kv_tok[rel * NX] = kv[0, rel * 2 * cols : (rel + 1) * 2 * cols, mine]
    w_c.wait_recv()
    tok = kv_tok[...].reshape(-1, rows).T
    inner = jnp.zeros((rows, 1), F32)
    inv = inv_ref[...]
    chunk = min(256, width)
    for at in range(0, width, chunk):
        here = slice(at, at + chunk)
        weights = w_all[:, :, here].reshape(-1, chunk)
        grad = jnp.dot(tok, weights, preferred_element_type=F32)
        unit = hid[:, here].astype(F32) * inv
        normed_grad[:, here] = grad
        both = grad * unit
        inner = inner + jnp.sum(both * gain[:, here], axis=-1, keepdims=True)
        total = jnp.sum(both, axis=0, keepdims=True)
        part = width // (NX * NC)
        for i in range(chunk // part):
            ga[at // part + i] = total[:, i * part : (i + 1) * part]
    inner = inner * (1.0 / width)

    g_1 = []
    me = x * NC + c
    for i, (dx, dc) in enumerate(xc):
        to = ((x + dx) % NX) * NC + (c + dc) % NC
        g_1.append(go(remote(ga.at[to], g1.at[me], g1_s.at[i], g1_r.at[i], device(dc=dc, dx=dx))))
    g1[me] = ga[me]

    loads[8].wait()
    for at in range(0, width, chunk):
        here = slice(at, at + chunk)
        unit = hid[:, here].astype(F32) * inv
        scaled = normed_grad[:, here] * gain[:, here]
        out_ref[:, here] = (res[:, here].astype(F32) + inv * (scaled - unit * inner)).astype(BF16)

    for copy in g_1:
        copy.wait_recv()
    g2[y] = jnp.sum(g1[...], axis=0)
    g_2 = [
        go(remote(g2.at[y], g2.at[y], g2_s.at[dy - 1], g2_r.at[dy - 1], device(dy=dy))) for dy in range(1, NY)
    ]
    for copy in g_2:
        copy.wait_recv()
    g3[z] = jnp.sum(g2[...], axis=0)
    g_3 = [
        go(remote(g3.at[z], g3.at[z], g3_s.at[dz - 1], g3_r.at[dz - 1], device(zz=(z + dz) % nz)))
        for dz in range(1, nz)
    ]

    for copy in z_all:
        copy.wait_recv()
    total = own_sum[aligned(zl, block), 0 : 2 * cols]
    for i in range(nz - 1):
        total = total + z_recv[i].astype(F32)
    total = total * scale
    kw_ref[...] = total[:, :cols]
    vw_ref[...] = total[:, cols:]

    for copy in g_3:
        copy.wait_recv()
    gf[me] = jnp.sum(g3[...], axis=0) * scale
    g_4 = [
        go(remote(gf.at[me], gf.at[me], g4_s.at[i], g4_r.at[i], device(dc=dc, dx=dx))) for i, (dx, dc) in enumerate(xc)
    ]
    for copy in g_4:
        copy.wait_recv()
    gain_out[...] = gf[...]
    for copy in sends:
        copy.wait_send()


def per_device(hidden_in, norm_gain, resid_grad, key_grad, value_grad, key_matrix, value_matrix):
    scale = 1.0 / math.sqrt(key_grad.shape[0] * lax.axis_size("dp"))
    rows, width = hidden_in.shape
    cols = key_matrix.shape[1]
    half = rows * NX
    block = width // (NC * NY * NZL)
    shard = width // NC // NY
    nz = NZL * NZH
    part = width // (NX * NC)
    dma = pltpu.SemaphoreType.DMA
    loose = pl.BlockSpec(memory_space=pltpu.HBM)
    vmem = pl.BlockSpec(memory_space=pltpu.VMEM)
    input_grad, key_sum, value_sum, gain_sum = pl.pallas_call(
        functools.partial(kernel, scale),
        out_shape=(
            jax.ShapeDtypeStruct((rows, width), BF16),
            jax.ShapeDtypeStruct((block, cols), F32),
            jax.ShapeDtypeStruct((block, cols), F32),
            jax.ShapeDtypeStruct((NX * NC, 1, part), F32),
        ),
        in_specs=[loose] * 7,
        out_specs=(vmem, vmem, vmem, vmem),
        scratch_shapes=[
            pltpu.VMEM((rows, width), BF16),
            pltpu.VMEM((rows, width), BF16),
            pltpu.VMEM((1, width), F32),
            pltpu.VMEM((rows, 1), F32),
            pltpu.VMEM((rows, width), BF16),
            pltpu.VMEM((NC, NY, shard, rows), BF16),
            pltpu.VMEM((NC, NY, shard, half), BF16),
            pltpu.VMEM((NC, NZH * 2 * cols, half), BF16),
            pltpu.VMEM((2 * cols, half), BF16),
            pltpu.VMEM((NZH * NX, 2 * cols, rows), BF16),
            pltpu.VMEM((NZH * NX, 2 * cols, width), BF16),
            pltpu.VMEM((rows, width), F32),
            pltpu.VMEM((NY - 1, shard, NZH * 2 * cols), BF16),
            pltpu.VMEM((NY - 1, shard, NZH * 2 * cols), BF16),
            pltpu.VMEM((shard, NZH * 2 * cols), F32),
            pltpu.VMEM((NZH, shard, 2 * cols), BF16),
            pltpu.VMEM((nz - 1, block, 2 * cols), BF16),
            pltpu.VMEM((NX * NC, 1, part), F32),
            pltpu.VMEM((NX * NC, 1, part), F32),
            pltpu.VMEM((NY, 1, part), F32),
            pltpu.VMEM((nz, 1, part), F32),
            pltpu.VMEM((NX * NC, 1, part), F32),
            dma((10,)),
            dma,
            dma,
            dma((2 * (NX - 1),)),
            dma((2 * (NX - 1),)),
            dma((2 * NY,)),
            dma((2 * NY,)),
            dma,
            dma,
            dma,
            dma,
            dma((2,)),
            dma((2,)),
            dma((2 * NX,)),
            dma((2 * NX,)),
            dma((NX * NC - 1,)),
            dma((NX * NC - 1,)),
            dma((NY - 1,)),
            dma((NY - 1,)),
            dma((nz - 1,)),
            dma((nz - 1,)),
            dma((NX * NC - 1,)),
            dma((NX * NC - 1,)),
            dma((NY - 1,)),
            dma((NY - 1,)),
            dma((nz - 1,)),
            dma((nz - 1,)),
            dma((NX * NC - 1,)),
            dma((NX * NC - 1,)),
        ],
        compiler_params=pltpu.CompilerParams(collective_id=0, has_side_effects=True, vmem_limit_bytes=62 * 1024 * 1024),
    )(
        hidden_in,
        norm_gain.reshape(1, width),
        resid_grad,
        key_grad.T,
        value_grad.T,
        key_matrix.T,
        value_matrix.T,
    )
    return input_grad, key_sum, value_sum, gain_sum.reshape(width)


def solution(mesh):
    return jax.shard_map(
        per_device,
        mesh=mesh,
        in_specs=(
            P(("dp", "seq"), None),
            P(),
            P(("dp", "seq"), None),
            P("dp", "seq"),
            P("dp", "seq"),
            P(None, "seq"),
            P(None, "seq"),
        ),
        out_specs=(P(("dp", "seq"), None), P("dp", "seq"), P("dp", "seq"), P()),
        check_vma=False,
    )
```

```python
import functools
import math

import jax
import jax.numpy as jnp
from jax import lax
from jax.experimental import pallas as pl
from jax.experimental.pallas import tpu as pltpu
from jax.sharding import PartitionSpec as P

EPSILON = 1e-05
MESH = pl.DeviceIdType.MESH
BF16, F32 = jnp.bfloat16, jnp.float32
NX, NY, NZL, NZH, NC = 4, 4, 8, 2, 2
SPLIT = 4
NT_DIMS = (((1,), (1,)), ((), ()))


def kernel(
    scale,
    hid_hbm,
    gain_hbm,
    res_hbm,
    kt_hbm,
    vt_hbm,
    wk_hbm,
    wv_hbm,
    out_ref,
    kw_ref,
    vw_ref,
    gain_out,
    hid,
    res,
    out_buf,
    gain,
    inv_ref,
    nrm,
    nt,
    ng_all,
    kv,
    kv_far,
    kv_tok,
    w_all,
    normed_grad,
    y_send,
    y_recv,
    own_sum,
    z_send,
    z_recv,
    wt,
    wt_far,
    gx,
    g3,
    gf,
    load_sem,
    wz_s,
    wz_r,
    wx_s,
    wx_r,
    wy_s,
    wy_r,
    wc_s,
    wc_r,
    kz_s,
    kz_r,
    kc_s,
    kc_r,
    kx_s,
    kx_r,
    n_s,
    n_r,
    y_s,
    y_r,
    z_s,
    z_r,
    wt_s,
    wt_r,
    gx_s,
    gx_r,
    g3_s,
    g3_r,
    g4_s,
    g4_r,
):
    dp, sq = lax.axis_index("dp"), lax.axis_index("seq")
    c, y, zl = dp % NC, (dp // NC) % NY, dp // (NC * NY)
    x, zh = sq % NX, sq // NX
    z = zh * NZL + zl
    nz = NZL * NZH
    rows, width = hid.shape
    cols = wk_hbm.shape[0]
    half = rows * NX
    piece = width // (NY * NC)

    def device(dc=0, dx=0, dy=0, zz=None):
        cc, xx, yy = (c + dc) % NC, (x + dx) % NX, (y + dy) % NY
        zz = z if zz is None else zz
        return ((zz % NZL) * NY + yy) * NC + cc, (zz // NZL) * NX + xx

    def remote(src, dst, ssem, rsem, to):
        return pltpu.make_async_remote_copy(
            src_ref=src, dst_ref=dst, send_sem=ssem, recv_sem=rsem, device_id=to, device_id_type=MESH
        )

    def aligned(index, size):
        return pl.ds(pl.multiple_of(index * size, size), size)

    near, far = aligned(zh, half), aligned(1 - zh, half)
    loads = [
        pltpu.make_async_copy(hid_hbm, hid, load_sem.at[0]),
        pltpu.make_async_copy(gain_hbm, gain, load_sem.at[1]),
        pltpu.make_async_copy(kt_hbm.at[:, far], kv_far.at[pl.ds(0, cols)], load_sem.at[2]),
        pltpu.make_async_copy(vt_hbm.at[:, far], kv_far.at[pl.ds(cols, cols)], load_sem.at[3]),
        pltpu.make_async_copy(wk_hbm, w_all.at[0, pl.ds(0, cols)], load_sem.at[4]),
        pltpu.make_async_copy(wv_hbm, w_all.at[0, pl.ds(cols, cols)], load_sem.at[5]),
        pltpu.make_async_copy(kt_hbm.at[:, near], kv.at[0, pl.ds(0, cols)], load_sem.at[6]),
        pltpu.make_async_copy(vt_hbm.at[:, near], kv.at[0, pl.ds(cols, cols)], load_sem.at[7]),
        pltpu.make_async_copy(res_hbm, res, load_sem.at[8]),
    ]
    for load in loads:
        load.start()

    barrier = pltpu.get_barrier_semaphore()
    xc = [(dx, dc) for dx in range(NX) for dc in range(NC) if dx or dc]
    peers = [device(dc=dc, dx=dx) for dx, dc in xc]
    yc = [(dy, dc) for dy in range(NY) for dc in range(NC) if dy or dc]
    peers += [device(dc=dc, dy=dy) for dy, dc in yc if dy]
    peers += [device(zz=(z + dz) % nz) for dz in range(1, nz)]
    for peer in peers:
        pl.semaphore_signal(barrier, inc=1, device_id=peer, device_id_type=MESH)

    loads[0].wait()
    loads[1].wait()
    step = 16
    for at in range(0, rows, step):
        wide = hid[at : at + step].astype(F32)
        inv = lax.rsqrt(jnp.mean(wide * wide, axis=-1, keepdims=True) + EPSILON)
        inv_ref[at : at + step] = inv
        nrm[at : at + step] = (wide * inv * gain[...]).astype(BF16)
    block = width // (NC * NY * NZL)
    lane = min(128, width)
    for at in range(0, width, lane):
        turned = nrm[:, at : at + lane].T
        for part in range(lane // block):
            b = at // block + part
            bc, by, bz = b % NC, (b // NC) % NY, b // (NC * NY)
            nt[bc, by, bz * block : (bz + 1) * block] = turned[part * block : (part + 1) * block]
    for load in loads[2:8]:
        load.wait()
    for at in range(0, width, lane):
        turned = w_all[0, :, at : at + lane].T
        for part in range(lane // block):
            b = at // block + part
            bc, by, bz = b % NC, (b // NC) % NY, b // (NC * NY)
            wt[bc, by, bz * block : (bz + 1) * block] = turned[part * block : (part + 1) * block]
    pl.semaphore_wait(barrier, len(peers))

    q = aligned(c * NY + y, piece)
    sends = []

    def go(copy):
        copy.start()
        sends.append(copy)
        return copy

    around = [(1, 0), (NX - 1, 1)]
    sides = [(1, 0), (NY - 1, 1)]

    share = NZL // 2
    deep = 2 * cols // share
    w_q = go(
        remote(
            w_all.at[0, aligned(share - 1 - zl % share, deep), q],
            w_all.at[NX, aligned(share - 1 - zl % share, deep), q],
            wz_s.at[0],
            wz_r.at[0],
            device(zz=nz - 1 - z),
        )
    )

    tall = piece // share

    def turned_send():
        rows_at = aligned(share - 1 - zl % share, tall)
        return go(remote(wt.at[c, y, rows_at], wt_far.at[rows_at], wt_s.at[0], wt_r.at[0], device(zz=nz - 1 - z)))

    def turned_share():
        wt_q.wait_recv()
        ref = wt_far.at[aligned(zl % share, tall)]
        return [
            go(remote(ref, ref, wt_s.at[d], wt_r.at[d], device(zz=z - zl % share + (zl + d) % share)))
            for d in range(1, share)
        ]

    def x_sends(rel):
        return [
            go(
                remote(
                    w_all.at[rel * NX, :, q],
                    w_all.at[rel * NX + dx, :, q],
                    wx_s.at[rel * NX + dx],
                    wx_r.at[rel * NX + dx],
                    device(dx=dx),
                )
            )
            for dx in range(1, NX)
        ]

    w_x = x_sends(0)
    k_z = go(remote(kv_far, kv.at[0, pl.ds(2 * cols, 2 * cols)], kz_s, kz_r, device(zz=(z + nz // 2) % nz)))
    wt_q = turned_send()
    k_c = go(remote(kv.at[0, pl.ds(0, 2 * cols)], kv.at[1, pl.ds(0, 2 * cols)], kc_s.at[0], kc_r.at[0], device(dc=1)))

    def token_sends(rel):
        return [
            go(
                remote(
                    kv.at[0, pl.ds(rel * 2 * cols, 2 * cols), aligned((x + dx) % NX, rows)],
                    kv_tok.at[rel * NX + dx],
                    kx_s.at[rel * NX + dx],
                    kx_r.at[rel * NX + dx],
                    device(dx=dx),
                )
            )
            for dx in range(1, NX)
        ]

    mine = aligned(x, rows)

    order = [d for d in (2, 1, 3, 0) if d < NY]

    def normed_sends(i):
        to = (y + order[i]) % NY
        return [
            go(
                remote(
                    nt.at[(c + dc) % NC, to],
                    ng_all.at[dc, to, :, mine],
                    n_s.at[(i * 2 + way) * NC + dc],
                    n_r.at[(i * 2 + way) * NC + dc],
                    device(dc=dc, dx=dx),
                )
            )
            for way, (dx, part) in enumerate(around)
            for dc in range(NC)
        ]

    def normed_pass(i):
        to = (y + order[i]) % NY
        deep = ng_all.shape[2] // 2
        out = []
        for way, (dx, part) in enumerate(around):
            for dc in range(NC):
                n_direct[i][way * NC + dc].wait_recv()
                ref = ng_all.at[dc, to, pl.ds(part * deep, deep), aligned((x - dx + NX) % NX, rows)]
                at = ((NY + i) * 2 + way) * NC + dc
                out.append(go(remote(ref, ref, n_s.at[at], n_r.at[at], device(dx=dx))))
        return out

    n_direct = [normed_sends(0)]
    n_core = go(remote(nt.at[(c + 1) % NC], ng_all.at[1, :, :, mine], n_s.at[4 * NY * NC], n_r.at[4 * NY * NC], device(dc=1)))
    own = pltpu.make_async_copy(nt.at[c], ng_all.at[0, :, :, mine], load_sem.at[9])
    own.start()
    k_x = token_sends(0)
    n_direct.append(normed_sends(1))

    def y_sends(rel):
        slots = pl.ds(rel * NX + (0 if rel else 1), NX if rel else NX - 1)
        first, second = [], []
        for turn, into in ((0, first), (1, second)):
            for way, (dy, part) in enumerate(sides):
                lanes = half_piece(c * NY + y, part if turn == 0 else 1 - part)
                at = rel * 6 + way * 2 + turn
                ref = w_all.at[slots, :, lanes]
                into.append(go(remote(ref, ref, wy_s.at[at], wy_r.at[at], device(dy=dy))))
        return first, second

    def half_piece(index, part):
        return pl.ds(pl.multiple_of(index * piece + part * (piece // 2), piece // 2), piece // 2)

    def y_pass(rel, first):
        slots = pl.ds(rel * NX + (0 if rel else 1), NX if rel else NX - 1)
        out = []
        for way, (dy, part) in enumerate(sides):
            first[way].wait_recv()
            lanes = half_piece(c * NY + (y - dy + NY) % NY, part)
            at = rel * 6 + 4 + way
            ref = w_all.at[slots, :, lanes]
            out.append(go(remote(ref, ref, wy_s.at[at], wy_r.at[at], device(dy=dy))))
        return out

    for copy in w_x:
        copy.wait_recv()
    w_y1, w_y2 = y_sends(0)
    w_q.wait_recv()
    ref = w_all.at[NX, aligned(zl % share, deep), q]
    w_z = [
        go(remote(ref, ref, wz_s.at[d], wz_r.at[d], device(zz=z - zl % share + (zl + d) % share)))
        for d in range(1, share)
    ]
    n_pass = [normed_pass(0)]
    for copy in w_z:
        copy.wait_recv()
    w_x2 = x_sends(1)
    n_direct.append(normed_sends(2))
    w_y3 = y_pass(0, w_y1)
    n_pass.append(normed_pass(1))
    n_direct.append(normed_sends(3))
    for copy in w_x2:
        copy.wait_recv()
    w_y4, w_y5 = y_sends(1)
    for copy in w_y2 + w_y3:
        copy.wait_recv()
    side = aligned(c, width // NC)
    ref = w_all.at[pl.ds(1, NX - 1), :, side]
    w_c = [go(remote(ref, ref, wc_s.at[0], wc_r.at[0], device(dc=1)))]

    k_z.wait_recv()
    k_c2 = go(
        remote(
            kv.at[0, pl.ds(2 * cols, 2 * cols)],
            kv.at[1, pl.ds(2 * cols, 2 * cols)],
            kc_s.at[1],
            kc_r.at[1],
            device(dc=1),
        )
    )
    k_x += token_sends(1)

    y_all = []

    def weight_chunk(i):
        dy = order[i]
        to = (y + dy) % NY
        for copy in n_pass[i]:
            copy.wait_recv()
        total = lax.dot_general(ng_all[0, to], kv[0], NT_DIMS, preferred_element_type=F32)
        total = total + lax.dot_general(ng_all[1, to], kv[1], NT_DIMS, preferred_element_type=F32)
        if dy:
            y_send[dy - 1] = total.astype(BF16)
            y_all.append(go(remote(y_send.at[dy - 1], y_recv.at[dy - 1], y_s.at[dy - 1], y_r.at[dy - 1], device(dy=dy))))
        else:
            own_sum[...] = total

    own.wait()
    for copy in [n_core, k_c, k_c2]:
        copy.wait_recv()
    w_t = turned_share()
    weight_chunk(0)
    n_pass.append(normed_pass(2))
    w_y6 = y_pass(1, w_y4)
    weight_chunk(1)
    n_pass.append(normed_pass(3))
    weight_chunk(2)
    weight_chunk(3)
    for copy in w_y5 + w_y6:
        copy.wait_recv()
    ref = w_all.at[pl.ds(NX, NX), :, side]
    w_c.append(go(remote(ref, ref, wc_s.at[1], wc_r.at[1], device(dc=1))))
    for copy in y_all:
        copy.wait_recv()
    total = own_sum[...]
    for i in range(NY - 1):
        total = total + y_recv[i].astype(F32)
    own_sum[...] = total
    for rel in range(NZH):
        z_send[rel] = total[:, rel * 2 * cols : (rel + 1) * 2 * cols].astype(BF16)
    z_all = []
    for dz in sorted(range(1, nz), key=lambda d: -min(d, nz - d)):
        to = (z + dz) % nz
        z_all.append(
            go(
                remote(
                    z_send.at[(to // NZL + zh) % NZH, aligned(to % NZL, block)],
                    z_recv.at[dz - 1],
                    z_s.at[dz - 1],
                    z_r.at[dz - 1],
                    device(zz=to),
                )
            )
        )

    for copy in w_t:
        copy.wait_recv()
    deepest = 2 * cols
    both = own_sum[:, :deepest] * wt[c, y].astype(F32) + own_sum[:, deepest:] * wt_far[...].astype(F32)
    gx[x] = jnp.sum(both.T, axis=0, keepdims=True)
    g_1 = [go(remote(gx.at[x], gx.at[x], gx_s.at[dx - 1], gx_r.at[dx - 1], device(dx=dx))) for dx in range(1, NX)]
    for copy in g_1:
        copy.wait_recv()
    g3[z] = jnp.sum(gx[...], axis=0)
    g_3 = [
        go(remote(g3.at[z], g3.at[z], g3_s.at[dz - 1], g3_r.at[dz - 1], device(zz=(z + dz) % nz)))
        for dz in range(1, nz)
    ]
    for copy in k_x:
        copy.wait_recv()
    for rel in range(NZH):
        kv_tok[rel * NX] = kv[0, rel * 2 * cols : (rel + 1) * 2 * cols, mine]
    tok = kv_tok[...].reshape(-1, rows).T
    inner = jnp.zeros((rows, 1), F32)
    inv = inv_ref[...]
    chunk = min(256, width // NC)
    for dc in range(NC):
        if dc:
            for copy in w_c:
                copy.wait_recv()
        for i in range(width // NC // chunk):
            at = ((c + dc) % NC) * (width // NC // chunk) + i
            here = aligned(at, chunk)
            weights = w_all[:, :, here].reshape(-1, chunk)
            grad = jnp.dot(tok, weights, preferred_element_type=F32)
            unit = hid[:, here].astype(F32) * inv
            normed_grad[:, here] = grad
            both = grad * unit
            inner = inner + jnp.sum(both * gain[:, here], axis=-1, keepdims=True)
    inner = inner * (1.0 / width)

    loads[8].wait()
    for at in range(0, width, chunk):
        here = slice(at, at + chunk)
        unit = hid[:, here].astype(F32) * inv
        scaled = normed_grad[:, here] * gain[:, here]
        out_buf[:, here] = (res[:, here].astype(F32) + inv * (scaled - unit * inner)).astype(BF16)
    stores = [pltpu.make_async_copy(out_buf, out_ref, load_sem.at[10])]
    for store in stores:
        store.start()
    for copy in z_all:
        copy.wait_recv()
    total = own_sum[aligned(zl, block), 0 : 2 * cols]
    for i in range(nz - 1):
        total = total + z_recv[i].astype(F32)
    total = total * scale
    kw_ref[...] = total[:, :cols]
    vw_ref[...] = total[:, cols:]

    for copy in g_3:
        copy.wait_recv()
    me = y * NC + c
    gf[me] = jnp.sum(g3[...], axis=0)
    g_4 = [
        go(remote(gf.at[me], gf.at[me], g4_s.at[i], g4_r.at[i], device(dc=dc, dy=dy))) for i, (dy, dc) in enumerate(yc)
    ]
    for copy in g_4:
        copy.wait_recv()
    for p in range(NY * NC):
        for b in range(NZL):
            at = (b * NY * NC + p) * block
            there = slice(at, at + block)
            gain_out[:, there] = gf[p][:, b * block : (b + 1) * block] / gain[:, there] * scale
    for store in stores:
        store.wait()
    for copy in sends:
        copy.wait_send()


def hand_over(grad, key, value, gain, grad_out, key_out, value_out, gain_out, held, in_sem, out_sem):
    deep = grad.shape[0] // SPLIT
    ins, outs = [], []
    for i in range(SPLIT):
        rows = pl.ds(i * deep, deep)
        ins.append(pltpu.make_async_copy(grad.at[rows], held.at[rows], in_sem.at[i]))
        outs.append(pltpu.make_async_copy(held.at[rows], grad_out.at[rows], out_sem.at[i]))
    for copy in ins:
        copy.start()
    for src, dst in ((key, key_out), (value, value_out), (gain, gain_out)):
        dst[...] = src[...]
    for first, second in zip(ins, outs):
        first.wait()
        second.start()
    for copy in outs:
        copy.wait()


def per_device(hidden_in, norm_gain, resid_grad, key_grad, value_grad, key_matrix, value_matrix):
    scale = 1.0 / math.sqrt(key_grad.shape[0] * lax.axis_size("dp"))
    rows, width = hidden_in.shape
    cols = key_matrix.shape[1]
    half = rows * NX
    block = width // (NC * NY * NZL)
    shard = width // NC // NY
    nz = NZL * NZH
    dma = pltpu.SemaphoreType.DMA
    loose = pl.BlockSpec(memory_space=pltpu.HBM)
    vmem = pl.BlockSpec(memory_space=pltpu.VMEM)
    input_grad, key_sum, value_sum, gain_sum = pl.pallas_call(
        functools.partial(kernel, scale),
        out_shape=(
            jax.ShapeDtypeStruct((rows, width), BF16),
            jax.ShapeDtypeStruct((block, cols), F32),
            jax.ShapeDtypeStruct((block, cols), F32),
            jax.ShapeDtypeStruct((1, width), F32),
        ),
        in_specs=[loose] * 7,
        out_specs=(loose, vmem, vmem, vmem),
        scratch_shapes=[
            pltpu.VMEM((rows, width), BF16),
            pltpu.VMEM((rows, width), BF16),
            pltpu.VMEM((rows, width), BF16),
            pltpu.VMEM((1, width), F32),
            pltpu.VMEM((rows, 1), F32),
            pltpu.VMEM((rows, width), BF16),
            pltpu.VMEM((NC, NY, shard, rows), BF16),
            pltpu.VMEM((NC, NY, shard, half), BF16),
            pltpu.VMEM((NC, NZH * 2 * cols, half), BF16),
            pltpu.VMEM((2 * cols, half), BF16),
            pltpu.VMEM((NZH * NX, 2 * cols, rows), BF16),
            pltpu.VMEM((NZH * NX, 2 * cols, width), BF16),
            pltpu.VMEM((rows, width), F32),
            pltpu.VMEM((NY - 1, shard, NZH * 2 * cols), BF16),
            pltpu.VMEM((NY - 1, shard, NZH * 2 * cols), BF16),
            pltpu.VMEM((shard, NZH * 2 * cols), F32),
            pltpu.VMEM((NZH, shard, 2 * cols), BF16),
            pltpu.VMEM((nz - 1, block, 2 * cols), BF16),
            pltpu.VMEM((NC, NY, shard, 2 * cols), BF16),
            pltpu.VMEM((shard, 2 * cols), BF16),
            pltpu.VMEM((NX, 1, shard), F32),
            pltpu.VMEM((nz, 1, shard), F32),
            pltpu.VMEM((NY * NC, 1, shard), F32),
            dma((11,)),
            dma((NZL // 2,)),
            dma((NZL // 2,)),
            dma((2 * NX,)),
            dma((2 * NX,)),
            dma((12,)),
            dma((12,)),
            dma((2,)),
            dma((2,)),
            dma,
            dma,
            dma((2,)),
            dma((2,)),
            dma((2 * NX,)),
            dma((2 * NX,)),
            dma((4 * NY * NC + 1,)),
            dma((4 * NY * NC + 1,)),
            dma((NY - 1,)),
            dma((NY - 1,)),
            dma((nz - 1,)),
            dma((nz - 1,)),
            dma((NZL // 2,)),
            dma((NZL // 2,)),
            dma((NX - 1,)),
            dma((NX - 1,)),
            dma((nz - 1,)),
            dma((nz - 1,)),
            dma((NY * NC - 1,)),
            dma((NY * NC - 1,)),
        ],
        compiler_params=pltpu.CompilerParams(collective_id=0, has_side_effects=True, vmem_limit_bytes=62 * 1024 * 1024),
    )(
        hidden_in,
        norm_gain.reshape(1, width),
        resid_grad,
        key_grad.T,
        value_grad.T,
        key_matrix.T,
        value_matrix.T,
    )
    done = (input_grad, key_sum, value_sum, gain_sum)
    input_grad, key_sum, value_sum, gain_sum = pl.pallas_call(
        hand_over,
        out_shape=tuple(jax.ShapeDtypeStruct(a.shape, a.dtype) for a in done),
        in_specs=[loose] + [vmem] * 3,
        out_specs=(loose,) + (vmem,) * 3,
        scratch_shapes=[pltpu.VMEM((rows, width), BF16), dma((SPLIT,)), dma((SPLIT,))],
    )(*done)
    return input_grad, key_sum, value_sum, gain_sum.reshape(width)


def solution(mesh):
    return jax.shard_map(
        per_device,
        mesh=mesh,
        in_specs=(
            P(("dp", "seq"), None),
            P(),
            P(("dp", "seq"), None),
            P("dp", "seq"),
            P("dp", "seq"),
            P(None, "seq"),
            P(None, "seq"),
        ),
        out_specs=(P(("dp", "seq"), None), P("dp", "seq"), P("dp", "seq"), P()),
        check_vma=False,
    )
```

```python
import functools
import math

import jax
import jax.numpy as jnp
from jax import lax
from jax.experimental import pallas as pl
from jax.experimental.pallas import tpu as pltpu
from jax.sharding import PartitionSpec as P

EPSILON = 1e-05
MESH = pl.DeviceIdType.MESH
BF16, F32 = jnp.bfloat16, jnp.float32
NX, NY, NZL, NZH, NC = 4, 4, 8, 2, 2
SPLIT = 4
NT_DIMS = (((1,), (1,)), ((), ()))


def kernel(
    scale,
    hid_hbm,
    gain_hbm,
    res_hbm,
    kt_hbm,
    vt_hbm,
    wk_hbm,
    wv_hbm,
    out_ref,
    kw_ref,
    vw_ref,
    gain_out,
    hid,
    res,
    out_buf,
    gain,
    inv_ref,
    nrm,
    nt,
    ng_all,
    kv,
    kv_far,
    kv_tok,
    w_all,
    normed_grad,
    y_send,
    y_recv,
    own_sum,
    z_send,
    z_recv,
    wt,
    wt_far,
    gx,
    g3,
    gf,
    load_sem,
    wz_s,
    wz_r,
    wx_s,
    wx_r,
    wy_s,
    wy_r,
    wc_s,
    wc_r,
    kz_s,
    kz_r,
    kc_s,
    kc_r,
    kx_s,
    kx_r,
    n_s,
    n_r,
    y_s,
    y_r,
    z_s,
    z_r,
    wt_s,
    wt_r,
    gx_s,
    gx_r,
    g3_s,
    g3_r,
    g4_s,
    g4_r,
):
    dp, sq = lax.axis_index("dp"), lax.axis_index("seq")
    c, y, zl = dp % NC, (dp // NC) % NY, dp // (NC * NY)
    x, zh = sq % NX, sq // NX
    z = zh * NZL + zl
    nz = NZL * NZH
    rows, width = hid.shape
    cols = wk_hbm.shape[0]
    half = rows * NX
    piece = width // (NY * NC)

    def device(dc=0, dx=0, dy=0, zz=None):
        cc, xx, yy = (c + dc) % NC, (x + dx) % NX, (y + dy) % NY
        zz = z if zz is None else zz
        return ((zz % NZL) * NY + yy) * NC + cc, (zz // NZL) * NX + xx

    def remote(src, dst, ssem, rsem, to):
        return pltpu.make_async_remote_copy(
            src_ref=src, dst_ref=dst, send_sem=ssem, recv_sem=rsem, device_id=to, device_id_type=MESH
        )

    def aligned(index, size):
        return pl.ds(pl.multiple_of(index * size, size), size)

    near, far = aligned(zh, half), aligned(1 - zh, half)
    loads = [
        pltpu.make_async_copy(hid_hbm, hid, load_sem.at[0]),
        pltpu.make_async_copy(gain_hbm, gain, load_sem.at[1]),
        pltpu.make_async_copy(kt_hbm.at[:, far], kv_far.at[pl.ds(0, cols)], load_sem.at[2]),
        pltpu.make_async_copy(vt_hbm.at[:, far], kv_far.at[pl.ds(cols, cols)], load_sem.at[3]),
        pltpu.make_async_copy(wk_hbm, w_all.at[0, pl.ds(0, cols)], load_sem.at[4]),
        pltpu.make_async_copy(wv_hbm, w_all.at[0, pl.ds(cols, cols)], load_sem.at[5]),
        pltpu.make_async_copy(kt_hbm.at[:, near], kv.at[0, pl.ds(0, cols)], load_sem.at[6]),
        pltpu.make_async_copy(vt_hbm.at[:, near], kv.at[0, pl.ds(cols, cols)], load_sem.at[7]),
        pltpu.make_async_copy(res_hbm, res, load_sem.at[8]),
    ]
    for load in loads:
        load.start()

    barrier = pltpu.get_barrier_semaphore()
    xc = [(dx, dc) for dx in range(NX) for dc in range(NC) if dx or dc]
    peers = [device(dc=dc, dx=dx) for dx, dc in xc]
    yc = [(dy, dc) for dy in range(NY) for dc in range(NC) if dy or dc]
    peers += [device(dc=dc, dy=dy) for dy, dc in yc if dy]
    peers += [device(zz=(z + dz) % nz) for dz in range(1, nz)]
    for peer in peers:
        pl.semaphore_signal(barrier, inc=1, device_id=peer, device_id_type=MESH)

    loads[0].wait()
    loads[1].wait()
    step = 16
    for at in range(0, rows, step):
        wide = hid[at : at + step].astype(F32)
        inv = lax.rsqrt(jnp.mean(wide * wide, axis=-1, keepdims=True) + EPSILON)
        inv_ref[at : at + step] = inv
        nrm[at : at + step] = (wide * inv * gain[...]).astype(BF16)
    block = width // (NC * NY * NZL)
    lane = min(128, width)
    for at in range(0, width, lane):
        turned = nrm[:, at : at + lane].T
        for part in range(lane // block):
            b = at // block + part
            bc, by, bz = b % NC, (b // NC) % NY, b // (NC * NY)
            nt[bc, by, bz * block : (bz + 1) * block] = turned[part * block : (part + 1) * block]
    for load in loads[2:8]:
        load.wait()
    for at in range(0, width, lane):
        turned = w_all[0, :, at : at + lane].T
        for part in range(lane // block):
            b = at // block + part
            bc, by, bz = b % NC, (b // NC) % NY, b // (NC * NY)
            wt[bc, by, bz * block : (bz + 1) * block] = turned[part * block : (part + 1) * block]
    pl.semaphore_wait(barrier, len(peers))

    q = aligned(c * NY + y, piece)
    sends = []

    def go(copy):
        copy.start()
        sends.append(copy)
        return copy

    around = [(1, 0), (NX - 1, 1)]
    sides = [(1, 0), (NY - 1, 1)]

    share = NZL // 2
    deep = 2 * cols // share
    w_q = go(
        remote(
            w_all.at[0, aligned(share - 1 - zl % share, deep), q],
            w_all.at[NX, aligned(share - 1 - zl % share, deep), q],
            wz_s.at[0],
            wz_r.at[0],
            device(zz=nz - 1 - z),
        )
    )

    tall = piece // share

    def turned_send():
        rows_at = aligned(share - 1 - zl % share, tall)
        return go(remote(wt.at[c, y, rows_at], wt_far.at[rows_at], wt_s.at[0], wt_r.at[0], device(zz=nz - 1 - z)))

    def turned_share():
        wt_q.wait_recv()
        ref = wt_far.at[aligned(zl % share, tall)]
        return [
            go(remote(ref, ref, wt_s.at[d], wt_r.at[d], device(zz=z - zl % share + (zl + d) % share)))
            for d in range(1, share)
        ]

    def x_sends(rel):
        return [
            go(
                remote(
                    w_all.at[rel * NX, :, q],
                    w_all.at[rel * NX + dx, :, q],
                    wx_s.at[rel * NX + dx],
                    wx_r.at[rel * NX + dx],
                    device(dx=dx),
                )
            )
            for dx in range(1, NX)
        ]

    w_x = x_sends(0)
    k_z = go(remote(kv_far, kv.at[0, pl.ds(2 * cols, 2 * cols)], kz_s, kz_r, device(zz=(z + nz // 2) % nz)))
    wt_q = turned_send()
    k_c = go(remote(kv.at[0, pl.ds(0, 2 * cols)], kv.at[1, pl.ds(0, 2 * cols)], kc_s.at[0], kc_r.at[0], device(dc=1)))

    def token_sends(rel):
        return [
            go(
                remote(
                    kv.at[0, pl.ds(rel * 2 * cols, 2 * cols), aligned((x + dx) % NX, rows)],
                    kv_tok.at[rel * NX + dx],
                    kx_s.at[rel * NX + dx],
                    kx_r.at[rel * NX + dx],
                    device(dx=dx),
                )
            )
            for dx in range(1, NX)
        ]

    mine = aligned(x, rows)

    order = [d for d in (2, 1, 3, 0) if d < NY]

    def normed_sends(i):
        to = (y + order[i]) % NY
        return [
            go(
                remote(
                    nt.at[(c + dc) % NC, to],
                    ng_all.at[dc, to, :, mine],
                    n_s.at[(i * 2 + way) * NC + dc],
                    n_r.at[(i * 2 + way) * NC + dc],
                    device(dc=dc, dx=dx),
                )
            )
            for way, (dx, part) in enumerate(around)
            for dc in range(NC)
        ]

    def normed_pass(i):
        to = (y + order[i]) % NY
        deep = ng_all.shape[2] // 2
        out = []
        for way, (dx, part) in enumerate(around):
            for dc in range(NC):
                n_direct[i][way * NC + dc].wait_recv()
                ref = ng_all.at[dc, to, pl.ds(part * deep, deep), aligned((x - dx + NX) % NX, rows)]
                at = ((NY + i) * 2 + way) * NC + dc
                out.append(go(remote(ref, ref, n_s.at[at], n_r.at[at], device(dx=dx))))
        return out

    n_direct = [normed_sends(0)]
    n_core = go(remote(nt.at[(c + 1) % NC], ng_all.at[1, :, :, mine], n_s.at[4 * NY * NC], n_r.at[4 * NY * NC], device(dc=1)))
    own = pltpu.make_async_copy(nt.at[c], ng_all.at[0, :, :, mine], load_sem.at[9])
    own.start()
    k_x = token_sends(0)
    n_direct.append(normed_sends(1))

    def y_sends(rel):
        slots = pl.ds(rel * NX + (0 if rel else 1), NX if rel else NX - 1)
        first, second = [], []
        for turn, into in ((0, first), (1, second)):
            for way, (dy, part) in enumerate(sides):
                lanes = half_piece(c * NY + y, part if turn == 0 else 1 - part)
                at = rel * 6 + way * 2 + turn
                ref = w_all.at[slots, :, lanes]
                into.append(go(remote(ref, ref, wy_s.at[at], wy_r.at[at], device(dy=dy))))
        return first, second

    def half_piece(index, part):
        return pl.ds(pl.multiple_of(index * piece + part * (piece // 2), piece // 2), piece // 2)

    def y_pass(rel, first):
        slots = pl.ds(rel * NX + (0 if rel else 1), NX if rel else NX - 1)
        out = []
        for way, (dy, part) in enumerate(sides):
            first[way].wait_recv()
            lanes = half_piece(c * NY + (y - dy + NY) % NY, part)
            at = rel * 6 + 4 + way
            ref = w_all.at[slots, :, lanes]
            out.append(go(remote(ref, ref, wy_s.at[at], wy_r.at[at], device(dy=dy))))
        return out

    for copy in w_x:
        copy.wait_recv()
    w_y1, w_y2 = y_sends(0)
    w_q.wait_recv()
    ref = w_all.at[NX, aligned(zl % share, deep), q]
    w_z = [
        go(remote(ref, ref, wz_s.at[d], wz_r.at[d], device(zz=z - zl % share + (zl + d) % share)))
        for d in range(1, share)
    ]
    n_pass = [normed_pass(0)]
    n_direct.append(normed_sends(2))
    w_y3 = y_pass(0, w_y1)
    n_pass.append(normed_pass(1))
    n_direct.append(normed_sends(3))
    for copy in w_z:
        copy.wait_recv()
    w_x2 = x_sends(1)
    for copy in w_y2 + w_y3:
        copy.wait_recv()
    side = aligned(c, width // NC)
    ref = w_all.at[pl.ds(1, NX - 1), :, side]
    w_c = [go(remote(ref, ref, wc_s.at[0], wc_r.at[0], device(dc=1)))]

    k_z.wait_recv()
    k_c2 = go(
        remote(
            kv.at[0, pl.ds(2 * cols, 2 * cols)],
            kv.at[1, pl.ds(2 * cols, 2 * cols)],
            kc_s.at[1],
            kc_r.at[1],
            device(dc=1),
        )
    )
    k_x += token_sends(1)

    y_all = []

    def weight_chunk(i):
        dy = order[i]
        to = (y + dy) % NY
        for copy in n_pass[i]:
            copy.wait_recv()
        total = lax.dot_general(ng_all[0, to], kv[0], NT_DIMS, preferred_element_type=F32)
        total = total + lax.dot_general(ng_all[1, to], kv[1], NT_DIMS, preferred_element_type=F32)
        if dy:
            y_send[dy - 1] = total.astype(BF16)
            y_all.append(go(remote(y_send.at[dy - 1], y_recv.at[dy - 1], y_s.at[dy - 1], y_r.at[dy - 1], device(dy=dy))))
        else:
            own_sum[...] = total

    own.wait()
    for copy in [n_core, k_c, k_c2]:
        copy.wait_recv()
    w_t = turned_share()
    weight_chunk(0)
    n_pass.append(normed_pass(2))
    weight_chunk(1)
    n_pass.append(normed_pass(3))
    weight_chunk(2)
    for copy in w_x2:
        copy.wait_recv()
    w_y4, w_y5 = y_sends(1)
    weight_chunk(3)
    for copy in y_all:
        copy.wait_recv()
    total = own_sum[...]
    for i in range(NY - 1):
        total = total + y_recv[i].astype(F32)
    own_sum[...] = total
    for rel in range(NZH):
        z_send[rel] = total[:, rel * 2 * cols : (rel + 1) * 2 * cols].astype(BF16)
    z_all = []
    for dz in sorted(range(1, nz), key=lambda d: -min(d, nz - d)):
        to = (z + dz) % nz
        z_all.append(
            go(
                remote(
                    z_send.at[(to // NZL + zh) % NZH, aligned(to % NZL, block)],
                    z_recv.at[dz - 1],
                    z_s.at[dz - 1],
                    z_r.at[dz - 1],
                    device(zz=to),
                )
            )
        )

    for copy in w_t:
        copy.wait_recv()
    deepest = 2 * cols
    both = own_sum[:, :deepest] * wt[c, y].astype(F32) + own_sum[:, deepest:] * wt_far[...].astype(F32)
    gx[x] = jnp.sum(both.T, axis=0, keepdims=True)
    g_1 = [go(remote(gx.at[x], gx.at[x], gx_s.at[dx - 1], gx_r.at[dx - 1], device(dx=dx))) for dx in range(1, NX)]
    for copy in g_1:
        copy.wait_recv()
    g3[z] = jnp.sum(gx[...], axis=0)
    g_3 = [
        go(remote(g3.at[z], g3.at[z], g3_s.at[dz - 1], g3_r.at[dz - 1], device(zz=(z + dz) % nz)))
        for dz in range(1, nz)
    ]
    w_y6 = y_pass(1, w_y4)
    for copy in w_y5 + w_y6:
        copy.wait_recv()
    ref = w_all.at[pl.ds(NX, NX), :, side]
    w_c.append(go(remote(ref, ref, wc_s.at[1], wc_r.at[1], device(dc=1))))
    for copy in k_x:
        copy.wait_recv()
    for rel in range(NZH):
        kv_tok[rel * NX] = kv[0, rel * 2 * cols : (rel + 1) * 2 * cols, mine]
    tok = kv_tok[...].reshape(-1, rows).T
    inner = jnp.zeros((rows, 1), F32)
    inv = inv_ref[...]
    chunk = min(256, width // NC)
    for dc in range(NC):
        if dc:
            for copy in w_c:
                copy.wait_recv()
        for i in range(width // NC // chunk):
            at = ((c + dc) % NC) * (width // NC // chunk) + i
            here = aligned(at, chunk)
            weights = w_all[:, :, here].reshape(-1, chunk)
            grad = jnp.dot(tok, weights, preferred_element_type=F32)
            unit = hid[:, here].astype(F32) * inv
            normed_grad[:, here] = grad
            both = grad * unit
            inner = inner + jnp.sum(both * gain[:, here], axis=-1, keepdims=True)
    inner = inner * (1.0 / width)

    loads[8].wait()
    for at in range(0, width, chunk):
        here = slice(at, at + chunk)
        unit = hid[:, here].astype(F32) * inv
        scaled = normed_grad[:, here] * gain[:, here]
        out_buf[:, here] = (res[:, here].astype(F32) + inv * (scaled - unit * inner)).astype(BF16)
    stores = [pltpu.make_async_copy(out_buf, out_ref, load_sem.at[10])]
    for store in stores:
        store.start()
    for copy in z_all:
        copy.wait_recv()
    total = own_sum[aligned(zl, block), 0 : 2 * cols]
    for i in range(nz - 1):
        total = total + z_recv[i].astype(F32)
    total = total * scale
    kw_ref[...] = total[:, :cols]
    vw_ref[...] = total[:, cols:]

    for copy in g_3:
        copy.wait_recv()
    me = y * NC + c
    gf[me] = jnp.sum(g3[...], axis=0)
    g_4 = [
        go(remote(gf.at[me], gf.at[me], g4_s.at[i], g4_r.at[i], device(dc=dc, dy=dy))) for i, (dy, dc) in enumerate(yc)
    ]
    for copy in g_4:
        copy.wait_recv()
    gain_out[...] = gf[...]
    for store in stores:
        store.wait()
    for copy in sends:
        copy.wait_send()


def hand_over(scale, grad, key, value, gain, norm_gain, grad_out, key_out, value_out, gain_out, held, in_sem, out_sem):
    deep = grad.shape[0] // SPLIT
    ins, outs = [], []
    for i in range(SPLIT):
        rows = pl.ds(i * deep, deep)
        ins.append(pltpu.make_async_copy(grad.at[rows], held.at[rows], in_sem.at[i]))
        outs.append(pltpu.make_async_copy(held.at[rows], grad_out.at[rows], out_sem.at[i]))
    for copy in ins:
        copy.start()
    key_out[...] = key[...]
    value_out[...] = value[...]
    parts, block = gain.shape[0], gain.shape[2] // NZL
    for p in range(parts):
        for b in range(NZL):
            at = (b * parts + p) * block
            gain_out[:, at : at + block] = gain[p][:, b * block : (b + 1) * block] * scale
    for first, second in zip(ins, outs):
        first.wait()
        second.start()
    gain_out[...] = gain_out[...] / norm_gain[...]
    for copy in outs:
        copy.wait()


def per_device(hidden_in, norm_gain, resid_grad, key_grad, value_grad, key_matrix, value_matrix):
    scale = 1.0 / math.sqrt(key_grad.shape[0] * lax.axis_size("dp"))
    rows, width = hidden_in.shape
    cols = key_matrix.shape[1]
    half = rows * NX
    block = width // (NC * NY * NZL)
    shard = width // NC // NY
    nz = NZL * NZH
    dma = pltpu.SemaphoreType.DMA
    loose = pl.BlockSpec(memory_space=pltpu.HBM)
    vmem = pl.BlockSpec(memory_space=pltpu.VMEM)
    input_grad, key_sum, value_sum, gain_sum = pl.pallas_call(
        functools.partial(kernel, scale),
        out_shape=(
            jax.ShapeDtypeStruct((rows, width), BF16),
            jax.ShapeDtypeStruct((block, cols), F32),
            jax.ShapeDtypeStruct((block, cols), F32),
            jax.ShapeDtypeStruct((NY * NC, 1, shard), F32),
        ),
        in_specs=[loose] * 7,
        out_specs=(loose, vmem, vmem, vmem),
        scratch_shapes=[
            pltpu.VMEM((rows, width), BF16),
            pltpu.VMEM((rows, width), BF16),
            pltpu.VMEM((rows, width), BF16),
            pltpu.VMEM((1, width), F32),
            pltpu.VMEM((rows, 1), F32),
            pltpu.VMEM((rows, width), BF16),
            pltpu.VMEM((NC, NY, shard, rows), BF16),
            pltpu.VMEM((NC, NY, shard, half), BF16),
            pltpu.VMEM((NC, NZH * 2 * cols, half), BF16),
            pltpu.VMEM((2 * cols, half), BF16),
            pltpu.VMEM((NZH * NX, 2 * cols, rows), BF16),
            pltpu.VMEM((NZH * NX, 2 * cols, width), BF16),
            pltpu.VMEM((rows, width), F32),
            pltpu.VMEM((NY - 1, shard, NZH * 2 * cols), BF16),
            pltpu.VMEM((NY - 1, shard, NZH * 2 * cols), BF16),
            pltpu.VMEM((shard, NZH * 2 * cols), F32),
            pltpu.VMEM((NZH, shard, 2 * cols), BF16),
            pltpu.VMEM((nz - 1, block, 2 * cols), BF16),
            pltpu.VMEM((NC, NY, shard, 2 * cols), BF16),
            pltpu.VMEM((shard, 2 * cols), BF16),
            pltpu.VMEM((NX, 1, shard), F32),
            pltpu.VMEM((nz, 1, shard), F32),
            pltpu.VMEM((NY * NC, 1, shard), F32),
            dma((11,)),
            dma((NZL // 2,)),
            dma((NZL // 2,)),
            dma((2 * NX,)),
            dma((2 * NX,)),
            dma((12,)),
            dma((12,)),
            dma((2,)),
            dma((2,)),
            dma,
            dma,
            dma((2,)),
            dma((2,)),
            dma((2 * NX,)),
            dma((2 * NX,)),
            dma((4 * NY * NC + 1,)),
            dma((4 * NY * NC + 1,)),
            dma((NY - 1,)),
            dma((NY - 1,)),
            dma((nz - 1,)),
            dma((nz - 1,)),
            dma((NZL // 2,)),
            dma((NZL // 2,)),
            dma((NX - 1,)),
            dma((NX - 1,)),
            dma((nz - 1,)),
            dma((nz - 1,)),
            dma((NY * NC - 1,)),
            dma((NY * NC - 1,)),
        ],
        compiler_params=pltpu.CompilerParams(collective_id=0, has_side_effects=True, vmem_limit_bytes=62 * 1024 * 1024),
    )(
        hidden_in,
        norm_gain.reshape(1, width),
        resid_grad,
        key_grad.T,
        value_grad.T,
        key_matrix.T,
        value_matrix.T,
    )
    done = (input_grad, key_sum, value_sum, gain_sum, norm_gain.reshape(1, width))
    input_grad, key_sum, value_sum, gain_sum = pl.pallas_call(
        functools.partial(hand_over, scale),
        out_shape=tuple(jax.ShapeDtypeStruct(a.shape, a.dtype) for a in done[:3] + done[4:]),
        in_specs=[loose] + [vmem] * 4,
        out_specs=(loose,) + (vmem,) * 3,
        scratch_shapes=[pltpu.VMEM((rows, width), BF16), dma((SPLIT,)), dma((SPLIT,))],
    )(*done)
    return input_grad, key_sum, value_sum, gain_sum.reshape(width)


def solution(mesh):
    return jax.shard_map(
        per_device,
        mesh=mesh,
        in_specs=(
            P(("dp", "seq"), None),
            P(),
            P(("dp", "seq"), None),
            P("dp", "seq"),
            P("dp", "seq"),
            P(None, "seq"),
            P(None, "seq"),
        ),
        out_specs=(P(("dp", "seq"), None), P("dp", "seq"), P("dp", "seq"), P()),
        check_vma=False,
    )
```

```python
import functools
import math

import jax
import jax.numpy as jnp
from jax import lax
from jax.experimental import pallas as pl
from jax.experimental.pallas import tpu as pltpu
from jax.sharding import PartitionSpec as P

EPSILON = 1e-05
MESH = pl.DeviceIdType.MESH
BF16, F32 = jnp.bfloat16, jnp.float32
NX, NY, NZL, NZH, NC = 4, 4, 8, 2, 2
SPLIT = 8
NT_DIMS = (((1,), (1,)), ((), ()))


def kernel(
    scale,
    hid_hbm,
    gain_hbm,
    res_hbm,
    kt_hbm,
    vt_hbm,
    wk_hbm,
    wv_hbm,
    out_ref,
    kw_ref,
    vw_ref,
    gain_out,
    hid,
    res,
    out_buf,
    gain,
    inv_ref,
    nrm,
    nt,
    ng_all,
    kv,
    kv_far,
    kv_tok,
    w_all,
    normed_grad,
    y_send,
    y_recv,
    own_sum,
    z_send,
    z_recv,
    wt,
    wt_far,
    gx,
    g3,
    gf,
    load_sem,
    wz_s,
    wz_r,
    wx_s,
    wx_r,
    wy_s,
    wy_r,
    wc_s,
    wc_r,
    kz_s,
    kz_r,
    kc_s,
    kc_r,
    kx_s,
    kx_r,
    n_s,
    n_r,
    y_s,
    y_r,
    z_s,
    z_r,
    wt_s,
    wt_r,
    gx_s,
    gx_r,
    g3_s,
    g3_r,
    g4_s,
    g4_r,
):
    dp, sq = lax.axis_index("dp"), lax.axis_index("seq")
    c, y, zl = dp % NC, (dp // NC) % NY, dp // (NC * NY)
    x, zh = sq % NX, sq // NX
    z = zh * NZL + zl
    nz = NZL * NZH
    rows, width = hid.shape
    cols = wk_hbm.shape[0]
    half = rows * NX
    piece = width // (NY * NC)

    def device(dc=0, dx=0, dy=0, zz=None):
        cc, xx, yy = (c + dc) % NC, (x + dx) % NX, (y + dy) % NY
        zz = z if zz is None else zz
        return ((zz % NZL) * NY + yy) * NC + cc, (zz // NZL) * NX + xx

    def remote(src, dst, ssem, rsem, to):
        return pltpu.make_async_remote_copy(
            src_ref=src, dst_ref=dst, send_sem=ssem, recv_sem=rsem, device_id=to, device_id_type=MESH
        )

    def aligned(index, size):
        return pl.ds(pl.multiple_of(index * size, size), size)

    near, far = aligned(zh, half), aligned(1 - zh, half)
    loads = [
        pltpu.make_async_copy(hid_hbm, hid, load_sem.at[0]),
        pltpu.make_async_copy(gain_hbm, gain, load_sem.at[1]),
        pltpu.make_async_copy(kt_hbm.at[:, far], kv_far.at[pl.ds(0, cols)], load_sem.at[2]),
        pltpu.make_async_copy(vt_hbm.at[:, far], kv_far.at[pl.ds(cols, cols)], load_sem.at[3]),
        pltpu.make_async_copy(wk_hbm, w_all.at[0, pl.ds(0, cols)], load_sem.at[4]),
        pltpu.make_async_copy(wv_hbm, w_all.at[0, pl.ds(cols, cols)], load_sem.at[5]),
        pltpu.make_async_copy(kt_hbm.at[:, near], kv.at[0, pl.ds(0, cols)], load_sem.at[6]),
        pltpu.make_async_copy(vt_hbm.at[:, near], kv.at[0, pl.ds(cols, cols)], load_sem.at[7]),
        pltpu.make_async_copy(res_hbm, res, load_sem.at[8]),
    ]
    for load in loads:
        load.start()

    barrier = pltpu.get_barrier_semaphore()
    xc = [(dx, dc) for dx in range(NX) for dc in range(NC) if dx or dc]
    peers = [device(dc=dc, dx=dx) for dx, dc in xc]
    yc = [(dy, dc) for dy in range(NY) for dc in range(NC) if dy or dc]
    peers += [device(dc=dc, dy=dy) for dy, dc in yc if dy]
    peers += [device(zz=(z + dz) % nz) for dz in range(1, nz)]
    for peer in peers:
        pl.semaphore_signal(barrier, inc=1, device_id=peer, device_id_type=MESH)

    loads[0].wait()
    loads[1].wait()
    step = 16
    for at in range(0, rows, step):
        wide = hid[at : at + step].astype(F32)
        inv = lax.rsqrt(jnp.mean(wide * wide, axis=-1, keepdims=True) + EPSILON)
        inv_ref[at : at + step] = inv
        nrm[at : at + step] = (wide * inv * gain[...]).astype(BF16)
    block = width // (NC * NY * NZL)
    lane = min(128, width)
    for at in range(0, width, lane):
        turned = nrm[:, at : at + lane].T
        for part in range(lane // block):
            b = at // block + part
            bc, by, bz = b % NC, (b // NC) % NY, b // (NC * NY)
            nt[bc, by, bz * block : (bz + 1) * block] = turned[part * block : (part + 1) * block]
    for load in loads[2:8]:
        load.wait()
    for at in range(0, width, lane):
        turned = w_all[0, :, at : at + lane].T
        for part in range(lane // block):
            b = at // block + part
            bc, by, bz = b % NC, (b // NC) % NY, b // (NC * NY)
            wt[bc, by, bz * block : (bz + 1) * block] = turned[part * block : (part + 1) * block]
    pl.semaphore_wait(barrier, len(peers))

    q = aligned(c * NY + y, piece)
    sends = []

    def go(copy):
        copy.start()
        sends.append(copy)
        return copy

    around = [(1, 0), (NX - 1, 1)]
    sides = [(1, 0), (NY - 1, 1)]

    share = NZL // 2
    deep = 2 * cols // share
    w_q = go(
        remote(
            w_all.at[0, aligned(share - 1 - zl % share, deep), q],
            w_all.at[NX, aligned(share - 1 - zl % share, deep), q],
            wz_s.at[0],
            wz_r.at[0],
            device(zz=nz - 1 - z),
        )
    )

    tall = piece // share

    def turned_send():
        rows_at = aligned(share - 1 - zl % share, tall)
        return go(remote(wt.at[c, y, rows_at], wt_far.at[rows_at], wt_s.at[0], wt_r.at[0], device(zz=nz - 1 - z)))

    def turned_share():
        wt_q.wait_recv()
        ref = wt_far.at[aligned(zl % share, tall)]
        return [
            go(remote(ref, ref, wt_s.at[d], wt_r.at[d], device(zz=z - zl % share + (zl + d) % share)))
            for d in range(1, share)
        ]

    def x_sends(rel):
        return [
            go(
                remote(
                    w_all.at[rel * NX, :, q],
                    w_all.at[rel * NX + dx, :, q],
                    wx_s.at[rel * NX + dx],
                    wx_r.at[rel * NX + dx],
                    device(dx=dx),
                )
            )
            for dx in range(1, NX)
        ]

    w_x = x_sends(0)
    k_z = go(remote(kv_far, kv.at[0, pl.ds(2 * cols, 2 * cols)], kz_s, kz_r, device(zz=(z + nz // 2) % nz)))
    wt_q = turned_send()
    k_c = go(remote(kv.at[0, pl.ds(0, 2 * cols)], kv.at[1, pl.ds(0, 2 * cols)], kc_s.at[0], kc_r.at[0], device(dc=1)))

    def token_sends(rel):
        return [
            go(
                remote(
                    kv.at[0, pl.ds(rel * 2 * cols, 2 * cols), aligned((x + dx) % NX, rows)],
                    kv_tok.at[rel * NX + dx],
                    kx_s.at[rel * NX + dx],
                    kx_r.at[rel * NX + dx],
                    device(dx=dx),
                )
            )
            for dx in range(1, NX)
        ]

    mine = aligned(x, rows)

    order = [d for d in (2, 1, 3, 0) if d < NY]

    def normed_sends(i):
        to = (y + order[i]) % NY
        return [
            go(
                remote(
                    nt.at[(c + dc) % NC, to],
                    ng_all.at[dc, to, :, mine],
                    n_s.at[(i * 2 + way) * NC + dc],
                    n_r.at[(i * 2 + way) * NC + dc],
                    device(dc=dc, dx=dx),
                )
            )
            for way, (dx, part) in enumerate(around)
            for dc in range(NC)
        ]

    def normed_pass(i):
        to = (y + order[i]) % NY
        deep = ng_all.shape[2] // 2
        out = []
        for way, (dx, part) in enumerate(around):
            for dc in range(NC):
                n_direct[i][way * NC + dc].wait_recv()
                ref = ng_all.at[dc, to, pl.ds(part * deep, deep), aligned((x - dx + NX) % NX, rows)]
                at = ((NY + i) * 2 + way) * NC + dc
                out.append(go(remote(ref, ref, n_s.at[at], n_r.at[at], device(dx=dx))))
        return out

    n_direct = [normed_sends(0)]
    n_core = go(remote(nt.at[(c + 1) % NC], ng_all.at[1, :, :, mine], n_s.at[4 * NY * NC], n_r.at[4 * NY * NC], device(dc=1)))
    own = pltpu.make_async_copy(nt.at[c], ng_all.at[0, :, :, mine], load_sem.at[9])
    own.start()
    n_direct.append(normed_sends(1))

    def y_sends(rel):
        slots = pl.ds(rel * NX + (0 if rel else 1), NX if rel else NX - 1)
        first, second = [], []
        for turn, into in ((0, first), (1, second)):
            for way, (dy, part) in enumerate(sides):
                lanes = half_piece(c * NY + y, part if turn == 0 else 1 - part)
                at = rel * 6 + way * 2 + turn
                ref = w_all.at[slots, :, lanes]
                into.append(go(remote(ref, ref, wy_s.at[at], wy_r.at[at], device(dy=dy))))
        return first, second

    def half_piece(index, part):
        return pl.ds(pl.multiple_of(index * piece + part * (piece // 2), piece // 2), piece // 2)

    def y_pass(rel, first):
        slots = pl.ds(rel * NX + (0 if rel else 1), NX if rel else NX - 1)
        out = []
        for way, (dy, part) in enumerate(sides):
            first[way].wait_recv()
            lanes = half_piece(c * NY + (y - dy + NY) % NY, part)
            at = rel * 6 + 4 + way
            ref = w_all.at[slots, :, lanes]
            out.append(go(remote(ref, ref, wy_s.at[at], wy_r.at[at], device(dy=dy))))
        return out

    for copy in w_x:
        copy.wait_recv()
    w_y1, w_y2 = y_sends(0)
    w_q.wait_recv()
    ref = w_all.at[NX, aligned(zl % share, deep), q]
    w_z = [
        go(remote(ref, ref, wz_s.at[d], wz_r.at[d], device(zz=z - zl % share + (zl + d) % share)))
        for d in range(1, share)
    ]
    n_pass = [normed_pass(0)]
    n_direct.append(normed_sends(2))
    n_pass.append(normed_pass(1))
    n_direct.append(normed_sends(3))
    w_y3 = y_pass(0, w_y1)
    for copy in w_z:
        copy.wait_recv()
    w_x2 = x_sends(1)
    for copy in w_y2 + w_y3:
        copy.wait_recv()
    side = aligned(c, width // NC)
    ref = w_all.at[pl.ds(1, NX - 1), :, side]
    w_c = [go(remote(ref, ref, wc_s.at[0], wc_r.at[0], device(dc=1)))]

    k_z.wait_recv()
    k_c2 = go(
        remote(
            kv.at[0, pl.ds(2 * cols, 2 * cols)],
            kv.at[1, pl.ds(2 * cols, 2 * cols)],
            kc_s.at[1],
            kc_r.at[1],
            device(dc=1),
        )
    )

    y_all = []

    def weight_chunk(i):
        dy = order[i]
        to = (y + dy) % NY
        for copy in n_pass[i]:
            copy.wait_recv()
        total = lax.dot_general(ng_all[0, to], kv[0], NT_DIMS, preferred_element_type=F32)
        total = total + lax.dot_general(ng_all[1, to], kv[1], NT_DIMS, preferred_element_type=F32)
        if dy:
            y_send[dy - 1] = total.astype(BF16)
            y_all.append(go(remote(y_send.at[dy - 1], y_recv.at[dy - 1], y_s.at[dy - 1], y_r.at[dy - 1], device(dy=dy))))
        else:
            own_sum[...] = total

    own.wait()
    for copy in [n_core, k_c, k_c2]:
        copy.wait_recv()
    w_t = turned_share()
    weight_chunk(0)
    n_pass.append(normed_pass(2))
    weight_chunk(1)
    k_x = token_sends(0)
    k_x += token_sends(1)
    n_pass.append(normed_pass(3))
    weight_chunk(2)
    for copy in w_x2:
        copy.wait_recv()
    w_y4, w_y5 = y_sends(1)
    weight_chunk(3)
    for copy in y_all:
        copy.wait_recv()
    total = own_sum[...]
    for i in range(NY - 1):
        total = total + y_recv[i].astype(F32)
    own_sum[...] = total
    for rel in range(NZH):
        z_send[rel] = total[:, rel * 2 * cols : (rel + 1) * 2 * cols].astype(BF16)
    z_all = []
    for dz in sorted(range(1, nz), key=lambda d: -min(d, nz - d)):
        to = (z + dz) % nz
        z_all.append(
            go(
                remote(
                    z_send.at[(to // NZL + zh) % NZH, aligned(to % NZL, block)],
                    z_recv.at[dz - 1],
                    z_s.at[dz - 1],
                    z_r.at[dz - 1],
                    device(zz=to),
                )
            )
        )

    for copy in w_t:
        copy.wait_recv()
    deepest = 2 * cols
    both = own_sum[:, :deepest] * wt[c, y].astype(F32) + own_sum[:, deepest:] * wt_far[...].astype(F32)
    gx[x] = jnp.sum(both.T, axis=0, keepdims=True)
    g_1 = [go(remote(gx.at[x], gx.at[x], gx_s.at[dx - 1], gx_r.at[dx - 1], device(dx=dx))) for dx in range(1, NX)]
    for copy in g_1:
        copy.wait_recv()
    g3[z] = jnp.sum(gx[...], axis=0)
    g_3 = [
        go(remote(g3.at[z], g3.at[z], g3_s.at[dz - 1], g3_r.at[dz - 1], device(zz=(z + dz) % nz)))
        for dz in range(1, nz)
    ]
    w_y6 = y_pass(1, w_y4)
    for copy in w_y5 + w_y6:
        copy.wait_recv()
    ref = w_all.at[pl.ds(NX, NX), :, side]
    w_c.append(go(remote(ref, ref, wc_s.at[1], wc_r.at[1], device(dc=1))))
    for copy in k_x:
        copy.wait_recv()
    for rel in range(NZH):
        kv_tok[rel * NX] = kv[0, rel * 2 * cols : (rel + 1) * 2 * cols, mine]
    tok = kv_tok[...].reshape(-1, rows).T
    inner = jnp.zeros((rows, 1), F32)
    inv = inv_ref[...]
    chunk = min(256, width // NC)
    for dc in range(NC):
        if dc:
            for copy in w_c:
                copy.wait_recv()
        for i in range(width // NC // chunk):
            at = ((c + dc) % NC) * (width // NC // chunk) + i
            here = aligned(at, chunk)
            weights = w_all[:, :, here].reshape(-1, chunk)
            grad = jnp.dot(tok, weights, preferred_element_type=F32)
            unit = hid[:, here].astype(F32) * inv
            normed_grad[:, here] = grad
            both = grad * unit
            inner = inner + jnp.sum(both * gain[:, here], axis=-1, keepdims=True)
    inner = inner * (1.0 / width)

    for copy in z_all:
        copy.wait_recv()
    total = own_sum[aligned(zl, block), 0 : 2 * cols]
    for i in range(nz - 1):
        total = total + z_recv[i].astype(F32)
    total = total * scale
    kw_ref[...] = total[:, :cols]
    vw_ref[...] = total[:, cols:]

    for copy in g_3:
        copy.wait_recv()
    me = y * NC + c
    gf[me] = jnp.sum(g3[...], axis=0)
    g_4 = [
        go(remote(gf.at[me], gf.at[me], g4_s.at[i], g4_r.at[i], device(dc=dc, dy=dy))) for i, (dy, dc) in enumerate(yc)
    ]
    loads[8].wait()
    for at in range(0, width, chunk):
        here = slice(at, at + chunk)
        unit = hid[:, here].astype(F32) * inv
        scaled = normed_grad[:, here] * gain[:, here]
        out_buf[:, here] = (res[:, here].astype(F32) + inv * (scaled - unit * inner)).astype(BF16)
    stores = [pltpu.make_async_copy(out_buf, out_ref, load_sem.at[10])]
    for store in stores:
        store.start()
    for copy in g_4:
        copy.wait_recv()
    gain_out[...] = gf[...]
    for store in stores:
        store.wait()
    for copy in sends:
        copy.wait_send()


def hand_over(scale, grad, key, value, gain, norm_gain, grad_out, key_out, value_out, gain_out, held, in_sem, out_sem):
    deep = grad.shape[0] // SPLIT
    ins, outs = [], []
    for i in range(SPLIT):
        rows = pl.ds(i * deep, deep)
        ins.append(pltpu.make_async_copy(grad.at[rows], held.at[rows], in_sem.at[i]))
        outs.append(pltpu.make_async_copy(held.at[rows], grad_out.at[rows], out_sem.at[i]))
    for copy in ins:
        copy.start()
    key_out[...] = key[...]
    value_out[...] = value[...]
    parts, block = gain.shape[0], gain.shape[2] // NZL
    for p in range(parts):
        for b in range(NZL):
            at = (b * parts + p) * block
            gain_out[:, at : at + block] = gain[p][:, b * block : (b + 1) * block] * scale
    for first, second in zip(ins, outs):
        first.wait()
        second.start()
    gain_out[...] = gain_out[...] / norm_gain[...]
    for copy in outs:
        copy.wait()


def per_device(hidden_in, norm_gain, resid_grad, key_grad, value_grad, key_matrix, value_matrix):
    scale = 1.0 / math.sqrt(key_grad.shape[0] * lax.axis_size("dp"))
    rows, width = hidden_in.shape
    cols = key_matrix.shape[1]
    half = rows * NX
    block = width // (NC * NY * NZL)
    shard = width // NC // NY
    nz = NZL * NZH
    dma = pltpu.SemaphoreType.DMA
    loose = pl.BlockSpec(memory_space=pltpu.HBM)
    vmem = pl.BlockSpec(memory_space=pltpu.VMEM)
    input_grad, key_sum, value_sum, gain_sum = pl.pallas_call(
        functools.partial(kernel, scale),
        out_shape=(
            jax.ShapeDtypeStruct((rows, width), BF16),
            jax.ShapeDtypeStruct((block, cols), F32),
            jax.ShapeDtypeStruct((block, cols), F32),
            jax.ShapeDtypeStruct((NY * NC, 1, shard), F32),
        ),
        in_specs=[loose] * 7,
        out_specs=(loose, vmem, vmem, vmem),
        scratch_shapes=[
            pltpu.VMEM((rows, width), BF16),
            pltpu.VMEM((rows, width), BF16),
            pltpu.VMEM((rows, width), BF16),
            pltpu.VMEM((1, width), F32),
            pltpu.VMEM((rows, 1), F32),
            pltpu.VMEM((rows, width), BF16),
            pltpu.VMEM((NC, NY, shard, rows), BF16),
            pltpu.VMEM((NC, NY, shard, half), BF16),
            pltpu.VMEM((NC, NZH * 2 * cols, half), BF16),
            pltpu.VMEM((2 * cols, half), BF16),
            pltpu.VMEM((NZH * NX, 2 * cols, rows), BF16),
            pltpu.VMEM((NZH * NX, 2 * cols, width), BF16),
            pltpu.VMEM((rows, width), F32),
            pltpu.VMEM((NY - 1, shard, NZH * 2 * cols), BF16),
            pltpu.VMEM((NY - 1, shard, NZH * 2 * cols), BF16),
            pltpu.VMEM((shard, NZH * 2 * cols), F32),
            pltpu.VMEM((NZH, shard, 2 * cols), BF16),
            pltpu.VMEM((nz - 1, block, 2 * cols), BF16),
            pltpu.VMEM((NC, NY, shard, 2 * cols), BF16),
            pltpu.VMEM((shard, 2 * cols), BF16),
            pltpu.VMEM((NX, 1, shard), F32),
            pltpu.VMEM((nz, 1, shard), F32),
            pltpu.VMEM((NY * NC, 1, shard), F32),
            dma((11,)),
            dma((NZL // 2,)),
            dma((NZL // 2,)),
            dma((2 * NX,)),
            dma((2 * NX,)),
            dma((12,)),
            dma((12,)),
            dma((2,)),
            dma((2,)),
            dma,
            dma,
            dma((2,)),
            dma((2,)),
            dma((2 * NX,)),
            dma((2 * NX,)),
            dma((4 * NY * NC + 1,)),
            dma((4 * NY * NC + 1,)),
            dma((NY - 1,)),
            dma((NY - 1,)),
            dma((nz - 1,)),
            dma((nz - 1,)),
            dma((NZL // 2,)),
            dma((NZL // 2,)),
            dma((NX - 1,)),
            dma((NX - 1,)),
            dma((nz - 1,)),
            dma((nz - 1,)),
            dma((NY * NC - 1,)),
            dma((NY * NC - 1,)),
        ],
        compiler_params=pltpu.CompilerParams(collective_id=0, has_side_effects=True, vmem_limit_bytes=62 * 1024 * 1024),
    )(
        hidden_in,
        norm_gain.reshape(1, width),
        resid_grad,
        key_grad.T,
        value_grad.T,
        key_matrix.T,
        value_matrix.T,
    )
    done = (input_grad, key_sum, value_sum, gain_sum, norm_gain.reshape(1, width))
    input_grad, key_sum, value_sum, gain_sum = pl.pallas_call(
        functools.partial(hand_over, scale),
        out_shape=tuple(jax.ShapeDtypeStruct(a.shape, a.dtype) for a in done[:3] + done[4:]),
        in_specs=[loose] + [vmem] * 4,
        out_specs=(loose,) + (vmem,) * 3,
        scratch_shapes=[pltpu.VMEM((rows, width), BF16), dma((SPLIT,)), dma((SPLIT,))],
    )(*done)
    return input_grad, key_sum, value_sum, gain_sum.reshape(width)


def solution(mesh):
    return jax.shard_map(
        per_device,
        mesh=mesh,
        in_specs=(
            P(("dp", "seq"), None),
            P(),
            P(("dp", "seq"), None),
            P("dp", "seq"),
            P("dp", "seq"),
            P(None, "seq"),
            P(None, "seq"),
        ),
        out_specs=(P(("dp", "seq"), None), P("dp", "seq"), P("dp", "seq"), P()),
        check_vma=False,
    )
```
